32 devices in a mesh: ctx: 8 (over z, core), rep: 4 (over y, x).
Axes of the slice: x: 2, y: 2, z: 4, core: 2. Of those that a mesh axis runs over, the one named last changes fastest.
Arguments:
- queries: bfloat16 [512, 8192], P(None, 'ctx'), may hold values from -6 to 6
- keys: bfloat16 [4096, 1024], P(('ctx', 'rep')), may hold values from -6 to 6
- values: bfloat16 [4096, 1024], P(('ctx', 'rep')), may hold values from -6 to 6
- forward_output: bfloat16 [512, 8192], P(None, 'ctx'), may hold values from -6 to 6
- output_gradient: bfloat16 [512, 8192], P(None, 'ctx'), may hold values from -6 to 6
- log_sum_norm: float32 [64, 512], P('ctx'), may hold values from 3 to 5
- block_attend_mask: int32 [64, 4, 32], P('ctx'), may hold values from 0 to 1, as said below
Outputs:
- grad_queries: bfloat16 [512, 8192], P('rep', 'ctx')
- key_gradient: bfloat16 [4096, 1024], P(('ctx', 'rep'))
- value_gradient: bfloat16 [4096, 1024], P(('ctx', 'rep'))
The draws below stay inside these ranges and needn't reach their ends.
Inputs may be any that keep to these rules, and one draw needn't show every extreme that they name: `block_attend_mask`: 1 where a query block of a query head attends a key block of 128 tokens, else 0; how many key blocks are attended differs from head to head.
All inputs are finite; a program needn't handle non-finite values.
Results may differ from the reference program's by a relative error of at most 0.007.
Values may be sent and summed in bfloat16 or wider, within the bound.
A program may use at most 64 MiB of HBM per device.

```python
import jax
import jax.numpy as jnp
from jax import lax

QUERY_HEADS = 64
KEY_VALUE_HEADS = 8
HEAD_SIZE = 128
BLK = 128
SLAB_QUERIES = 512
CONTEXT_TOKENS = 4096
QBLK = 4
KBLK = 32
N_CTX = 8


def draw_block_attend_mask(key, part):
    level_key, stripe_key, extra_key = jax.random.split(key, 3)
    levels = jax.random.randint(level_key, (QUERY_HEADS, 1, 1), 2, 9)
    stripes = (jax.random.randint(stripe_key, (QUERY_HEADS, 1, KBLK), 0, 32) < levels).astype(jnp.int32)
    extras = (jax.random.randint(extra_key, (QUERY_HEADS, QBLK, KBLK), 0, 32) < 1).astype(jnp.int32)
    return jnp.maximum(stripes, extras).astype(jnp.int32)


def shard_levels(own_key, shape, cuts, least, largest):
    factor_of, own = 1.0, jax.random.fold_in(own_key, 6)
    for axis_at, shards_of in cuts:
        steps = jnp.exp(jax.random.uniform(jax.random.fold_in(own, axis_at), (shards_of,), jnp.float32, least / len(cuts), largest / len(cuts)))
        factor_of = factor_of * jnp.repeat(steps, shape[axis_at] // shards_of).reshape([-1 if axis == axis_at else 1 for axis in range(len(shape))])
    return factor_of


def gaussian(key, extent, width, most, pieces=(), kind=jnp.bfloat16):
    array = width * jax.random.normal(key, extent, jnp.float32)
    if pieces:
        array = array * shard_levels(key, extent, pieces, -0.22, 0.18)
    return jnp.clip(array, -most, most).astype(kind)


def setup_inputs(seed: int = 0) -> dict:
    arg_keys = jax.random.split(jax.random.key(seed), 8)
    return {
        "queries": gaussian(arg_keys[0], (SLAB_QUERIES, QUERY_HEADS * HEAD_SIZE), 1.0, 6.0, ((1, 8),)),
        "keys": gaussian(arg_keys[1], (CONTEXT_TOKENS, KEY_VALUE_HEADS * HEAD_SIZE), 1.0, 6.0, ((0, 32),)),
        "values": gaussian(arg_keys[2], (CONTEXT_TOKENS, KEY_VALUE_HEADS * HEAD_SIZE), 1.0, 6.0, ((0, 32),)),
        "forward_output": gaussian(arg_keys[3], (SLAB_QUERIES, QUERY_HEADS * HEAD_SIZE), 1.0, 6.0, ((1, 8),)),
        "output_gradient": gaussian(arg_keys[4], (SLAB_QUERIES, QUERY_HEADS * HEAD_SIZE), 1.0, 6.0, ((1, 8),)),
        "log_sum_norm": jnp.clip(3.0 + 2.0 * jax.random.uniform(arg_keys[5], (QUERY_HEADS, SLAB_QUERIES), jnp.float32) ** shard_levels(arg_keys[5], (QUERY_HEADS, SLAB_QUERIES), ((0, 8),), -0.2, 0.2), 3.0, 5.0),
        "block_attend_mask": draw_block_attend_mask(jax.random.fold_in(arg_keys[7], 71), 0),
    }


def round_bf16(value):
    rounded = value.astype(jnp.bfloat16)
    return lax.optimization_barrier(rounded).astype(jnp.float32)


def pair_tree(parts):
    current = list(parts)
    level_count = len(current).bit_length() - 1
    for level in range(level_count):
        current = [round_bf16(current[index] + current[index + 1]) for index in range(0, len(current), 2)]
    return current[0]


def reference(queries, keys, values, forward_output, output_gradient, log_sum_norm, block_attend_mask):
    softmax_scale = HEAD_SIZE ** -0.5
    heads_dev = QUERY_HEADS // N_CTX
    group_members = QUERY_HEADS // KEY_VALUE_HEADS
    key_length = keys.shape[0]
    query_block_count = SLAB_QUERIES // BLK
    key_block_count = key_length // BLK
    highest = lax.Precision.HIGHEST
    full_queries = queries.reshape(SLAB_QUERIES, KEY_VALUE_HEADS, group_members, HEAD_SIZE).transpose(1, 2, 0, 3)
    full_output = forward_output.reshape(SLAB_QUERIES, KEY_VALUE_HEADS, group_members, HEAD_SIZE).transpose(1, 2, 0, 3)
    output_cotangent_full = output_gradient.reshape(SLAB_QUERIES, KEY_VALUE_HEADS, group_members, HEAD_SIZE).transpose(1, 2, 0, 3)
    full_keys = keys.reshape(key_length, KEY_VALUE_HEADS, HEAD_SIZE).transpose(1, 0, 2)
    full_values = values.reshape(key_length, KEY_VALUE_HEADS, HEAD_SIZE).transpose(1, 0, 2)
    full_norm = log_sum_norm.reshape(KEY_VALUE_HEADS, group_members, SLAB_QUERIES)
    full_mask = block_attend_mask.reshape(KEY_VALUE_HEADS, group_members, query_block_count, key_block_count)

    def one_group(items):
        query_g, output_g, cotan_g, key_g, value_g, norm_g, mask_g = items
        key_f32 = key_g.astype(jnp.float32)
        value_f32 = value_g.astype(jnp.float32)
        key_sets = []
        value_sets = []
        key_part = jnp.zeros((key_length, HEAD_SIZE), jnp.float32)
        value_part = jnp.zeros((key_length, HEAD_SIZE), jnp.float32)
        query_grads = []
        for head_index in range(group_members):
            query_h = query_g[head_index].astype(jnp.float32)
            output_h = output_g[head_index].astype(jnp.float32)
            cotan_h = cotan_g[head_index].astype(jnp.float32)
            mask_full = jnp.broadcast_to(mask_g[head_index][:, None, :, None].astype(jnp.float32), (query_block_count, BLK, key_block_count, BLK)).reshape(SLAB_QUERIES, key_length)
            row_dots = jnp.sum(cotan_h * output_h, axis=1)
            scores = jnp.dot(query_h, key_f32.T, precision=highest) * softmax_scale
            weights = jnp.exp(scores - norm_g[head_index][:, None]) * mask_full
            weights_b = round_bf16(weights)
            grad_weights = jnp.dot(cotan_h, value_f32.T, precision=highest)
            grad_scores = round_bf16(weights * (grad_weights - row_dots[:, None]))
            value_part = value_part + jnp.dot(weights_b.T, cotan_h, precision=highest)
            key_part = key_part + jnp.dot(grad_scores.T, query_h, precision=highest)
            query_grads.append((jnp.dot(grad_scores, key_f32, precision=highest) * softmax_scale).astype(jnp.bfloat16))
            if (head_index + 1) % heads_dev == 0:
                key_sets.append(round_bf16(key_part * softmax_scale))
                value_sets.append(round_bf16(value_part))
                key_part = jnp.zeros((key_length, HEAD_SIZE), jnp.float32)
                value_part = jnp.zeros((key_length, HEAD_SIZE), jnp.float32)
        key_total = pair_tree(key_sets)
        value_total = pair_tree(value_sets)
        return key_total.astype(jnp.bfloat16), value_total.astype(jnp.bfloat16), jnp.stack(query_grads)

    key_gradient_parts, value_gradient_parts, query_grads = lax.map(one_group, (full_queries, full_output, output_cotangent_full, full_keys, full_values, full_norm, full_mask))
    grad_queries = query_grads.reshape(QUERY_HEADS, SLAB_QUERIES, HEAD_SIZE).transpose(1, 0, 2).reshape(SLAB_QUERIES, QUERY_HEADS * HEAD_SIZE)
    key_gradient = key_gradient_parts.transpose(1, 0, 2).reshape(key_length, KEY_VALUE_HEADS * HEAD_SIZE)
    value_gradient = value_gradient_parts.transpose(1, 0, 2).reshape(key_length, KEY_VALUE_HEADS * HEAD_SIZE)
    return (grad_queries, key_gradient, value_gradient)
```

```python
import functools

import jax
import jax.numpy as jnp
from jax import lax
from jax.experimental import pallas as pl
from jax.experimental.pallas import tpu as pltpu
from jax.sharding import PartitionSpec as P

KEY_VALUE_HEADS = 8
HEAD_SIZE = 128
BLK = 128
MESH = pl.DeviceIdType.MESH
LOG2_E = 1.4426950408889634
MASKED = 1e30


def partner_of(index, step, count):
    total = 0
    bit = 1
    while bit < count:
        total = total + ((index // bit + step // bit) % 2) * bit
        bit *= 2
    return total


def kernel(
    n_ctx,
    n_rep,
    heads,
    group,
    keys,
    values,
    queries,
    fwd_out,
    grad_out,
    norm,
    mask,
    dq_out,
    dkv_out,
    q_v,
    o_v,
    g_v,
    qt_v,
    gt_v,
    norm_b,
    dots_b,
    kv_v,
    dk_acc,
    dv_acc,
    dq_acc,
    dkv_send,
    dq_send,
    dq_land,
    dkv_land,
    load_sem,
    kv_send_sem,
    kv_recv_sem,
    d_send_sem,
    d_recv_sem,
    q_send_sem,
    q_recv_sem,
):
    ctx = lax.axis_index("ctx")
    rep = lax.axis_index("rep")
    n_q = q_v.shape[0]
    rows = n_q // n_rep
    scale = HEAD_SIZE ** (-0.5)

    def head_cols(head):
        return pl.ds(pl.multiple_of(head * HEAD_SIZE, HEAD_SIZE), HEAD_SIZE)

    my_head = ctx // group
    my_cols = head_cols(my_head)

    loads = [
        pltpu.make_async_copy(keys.at[:, my_cols], kv_v.at[ctx, 0], load_sem.at[0]),
        pltpu.make_async_copy(values.at[:, my_cols], kv_v.at[ctx, 1], load_sem.at[1]),
        pltpu.make_async_copy(grad_out, g_v, load_sem.at[2]),
        pltpu.make_async_copy(fwd_out, o_v, load_sem.at[3]),
        pltpu.make_async_copy(queries, q_v, load_sem.at[4]),
    ]
    for load in loads:
        load.start()

    barrier = pltpu.get_barrier_semaphore()

    @pl.loop(1, n_ctx)
    def _(step):
        peer = partner_of(ctx, step, n_ctx)
        pl.semaphore_signal(barrier, inc=1, device_id=(peer, rep), device_id_type=MESH)

    @pl.loop(1, n_rep)
    def _(step):
        peer = partner_of(rep, step, n_rep)
        pl.semaphore_signal(barrier, inc=1, device_id=(ctx, peer), device_id_type=MESH)

    pl.semaphore_wait(barrier, n_ctx - 1 + n_rep - 1)

    def kv_copy(step, kind):
        peer = partner_of(ctx, step, n_ctx)
        source = (keys, values)[kind]
        return pltpu.make_async_remote_copy(
            src_ref=source.at[:, head_cols(peer // group)],
            dst_ref=kv_v.at[ctx, kind],
            send_sem=kv_send_sem.at[step, kind],
            recv_sem=kv_recv_sem.at[step, kind],
            device_id=(peer, rep),
            device_id_type=MESH,
        )

    def kv_arrival(step, kind):
        peer = partner_of(ctx, step, n_ctx)
        return pltpu.make_async_remote_copy(
            src_ref=(keys, values)[kind].at[:, my_cols],
            dst_ref=kv_v.at[peer, kind],
            send_sem=kv_send_sem.at[step, kind],
            recv_sem=kv_recv_sem.at[step, kind],
            device_id=(peer, rep),
            device_id_type=MESH,
        )

    @pl.loop(1, n_ctx)
    def _(step):
        kv_copy(step, 0).start()
        kv_copy(step, 1).start()

    for load in loads:
        load.wait()

    @pl.loop(0, heads)
    def _(head):
        cols = head_cols(head)
        g = g_v[:, cols]
        q = q_v[:, cols]
        dots = jnp.sum(g.astype(jnp.float32) * o_v[:, cols].astype(jnp.float32), axis=1, keepdims=True)
        dots_b[head] = jnp.broadcast_to(dots, (n_q, BLK))
        row = norm[pl.ds(head, 1), :] * LOG2_E
        norm_b[head] = jnp.broadcast_to(row, (BLK, n_q)).T
        qt_v[head] = q.T
        gt_v[head] = g.T
        dq_acc[head] = jnp.zeros((n_q, HEAD_SIZE), jnp.float32)

    def landing(source, kind):
        place = head_cols(source // group)
        if group == 1:
            return dkv_out.at[kind, :, place]
        return dkv_land.at[source % group, kind, :, place]

    def d_copy(step, kind):
        peer = partner_of(ctx, step, n_ctx)
        return pltpu.make_async_remote_copy(
            src_ref=dkv_send.at[step, kind],
            dst_ref=landing(ctx, kind),
            send_sem=d_send_sem.at[step, kind],
            recv_sem=d_recv_sem.at[step, kind],
            device_id=(peer, rep),
            device_id_type=MESH,
        )

    def d_arrival(step, kind):
        peer = partner_of(ctx, step, n_ctx)
        return pltpu.make_async_remote_copy(
            src_ref=dkv_send.at[step, kind],
            dst_ref=landing(peer, kind),
            send_sem=d_send_sem.at[step, kind],
            recv_sem=d_recv_sem.at[step, kind],
            device_id=(peer, rep),
            device_id_type=MESH,
        )

    def q_copy(step, head):
        peer = partner_of(rep, step, n_rep)
        at = pl.ds(pl.multiple_of(peer * rows, rows), rows)
        return pltpu.make_async_remote_copy(
            src_ref=dq_send.at[head, at],
            dst_ref=dq_land.at[step, head],
            send_sem=q_send_sem.at[step, head],
            recv_sem=q_recv_sem.at[step, head],
            device_id=(ctx, peer),
            device_id_type=MESH,
        )

    def compute(step, head):
        source = partner_of(ctx, step, n_ctx)
        cols = head_cols(head)
        k = kv_v[source, 0]
        v = kv_v[source, 1]
        q = q_v[:, cols]
        g = g_v[:, cols]
        nt = (((1,), (1,)), ((), ()))
        s = lax.dot_general(q, k, nt, preferred_element_type=jnp.float32)
        gw = lax.dot_general(g, v, nt, preferred_element_type=jnp.float32)
        key_block = source * n_rep + rep
        parts = []
        for qb in range(n_q // BLK):
            off = (1 - mask[head, qb, key_block]).astype(jnp.float32) * MASKED
            span = slice(qb * BLK, (qb + 1) * BLK)
            parts.append(jnp.exp2(s[span] * (scale * LOG2_E) - (norm_b[head, span, :] + off)))
        w = jnp.concatenate(parts, axis=0)
        p = w.astype(jnp.bfloat16)
        ds = (w * (gw - dots_b[head])).astype(jnp.bfloat16)
        dk_acc[...] += jnp.dot(qt_v[head], ds, preferred_element_type=jnp.float32)
        dv_acc[...] += jnp.dot(gt_v[head], p, preferred_element_type=jnp.float32)
        return dq_acc[head] + jnp.dot(ds, k, preferred_element_type=jnp.float32)

    def clear():
        dk_acc[...] = jnp.zeros_like(dk_acc)
        dv_acc[...] = jnp.zeros_like(dv_acc)

    clear()

    @pl.loop(0, heads)
    def _(head):
        dq_acc[head] = compute(0, head)

    own = [(dk_acc[...] * scale).T.astype(jnp.bfloat16), dv_acc[...].T.astype(jnp.bfloat16)]
    for kind in range(2):
        if group == 1:
            dkv_out[kind, :, my_cols] = own[kind]
        else:
            dkv_land[ctx % group, kind, :, my_cols] = own[kind]

    def arrive(step):
        kv_arrival(step, 0).wait_recv()
        kv_arrival(step, 1).wait_recv()
        clear()

    def give_back(step):
        dkv_send[step, 0] = (dk_acc[...] * scale).T.astype(jnp.bfloat16)
        d_copy(step, 0).start()
        dkv_send[step, 1] = dv_acc[...].T.astype(jnp.bfloat16)
        d_copy(step, 1).start()

    @pl.loop(1, n_ctx - 1)
    def _(step):
        arrive(step)

        @pl.loop(0, heads)
        def _(head):
            dq_acc[head] = compute(step, head)

        give_back(step)

    last = n_ctx - 1
    arrive(last)

    @pl.loop(0, heads)
    def _(head):
        total = compute(last, head) * scale
        dq_acc[head] = total
        dq_send[head] = total.astype(jnp.bfloat16)

        @pl.loop(1, n_rep)
        def _(step):
            q_copy(step, head).start()

    give_back(last)

    @pl.loop(1, n_ctx)
    def _(step):
        for kind in range(2):
            kv_copy(step, kind).wait_send()

    at = pl.ds(pl.multiple_of(rep * rows, rows), rows)

    @pl.loop(0, heads)
    def _(head):
        @pl.loop(1, n_rep)
        def _(step):
            q_copy(step, head).wait_recv()

        total = dq_acc[head, at, :]
        for step in range(1, n_rep):
            total = total + dq_land[step, head].astype(jnp.float32)
        dq_out[:, head_cols(head)] = total.astype(jnp.bfloat16)

    @pl.loop(1, n_ctx)
    def _(step):
        for kind in range(2):
            d_copy(step, kind).wait_send()
            d_arrival(step, kind).wait_recv()

    @pl.loop(0, heads)
    def _(head):
        @pl.loop(1, n_rep)
        def _(step):
            q_copy(step, head).wait_send()

    if group > 1:
        for kind in range(2):
            parts = [dkv_land[j, kind] for j in range(group)]
            while len(parts) > 1:
                parts = [
                    (parts[i].astype(jnp.float32) + parts[i + 1].astype(jnp.float32)).astype(jnp.bfloat16)
                    for i in range(0, len(parts), 2)
                ]
            dkv_out[kind] = parts[0]


def on_device(queries, keys, values, forward_output, output_gradient, log_sum_norm, block_attend_mask):
    n_ctx = lax.axis_size("ctx")
    n_rep = lax.axis_size("rep")
    group = n_ctx // KEY_VALUE_HEADS
    n_q, width = queries.shape
    heads = width // HEAD_SIZE
    rows = n_q // n_rep
    share = keys.shape[0]
    assert share == BLK
    any_spec = pl.BlockSpec(memory_space=pl.ANY)
    vmem = pl.BlockSpec(memory_space=pltpu.VMEM)
    smem = pl.BlockSpec(memory_space=pltpu.SMEM)
    bf16, f32 = jnp.bfloat16, jnp.float32
    land_group = group if group > 1 else 1
    land_cols = keys.shape[1] if group > 1 else HEAD_SIZE
    dq, dkv = pl.pallas_call(
        functools.partial(kernel, n_ctx, n_rep, heads, group),
        out_shape=(
            jax.ShapeDtypeStruct((rows, width), bf16),
            jax.ShapeDtypeStruct((2, share, keys.shape[1]), bf16),
        ),
        in_specs=[any_spec] * 5 + [vmem, smem],
        out_specs=(vmem, vmem),
        scratch_shapes=[
            pltpu.VMEM((n_q, width), bf16),
            pltpu.VMEM((n_q, width), bf16),
            pltpu.VMEM((n_q, width), bf16),
            pltpu.VMEM((heads, HEAD_SIZE, n_q), bf16),
            pltpu.VMEM((heads, HEAD_SIZE, n_q), bf16),
            pltpu.VMEM((heads, n_q, BLK), f32),
            pltpu.VMEM((heads, n_q, BLK), f32),
            pltpu.VMEM((n_ctx, 2, BLK, HEAD_SIZE), bf16),
            pltpu.VMEM((HEAD_SIZE, BLK), f32),
            pltpu.VMEM((HEAD_SIZE, BLK), f32),
            pltpu.VMEM((heads, n_q, HEAD_SIZE), f32),
            pltpu.VMEM((n_ctx, 2, BLK, HEAD_SIZE), bf16),
            pltpu.VMEM((heads, n_q, HEAD_SIZE), bf16),
            pltpu.VMEM((n_rep, heads, rows, HEAD_SIZE), bf16),
            pltpu.VMEM((land_group, 2, BLK, land_cols), bf16),
            pltpu.SemaphoreType.DMA((5,)),
            pltpu.SemaphoreType.DMA((n_ctx, 2)),
            pltpu.SemaphoreType.DMA((n_ctx, 2)),
            pltpu.SemaphoreType.DMA((n_ctx, 2)),
            pltpu.SemaphoreType.DMA((n_ctx, 2)),
            pltpu.SemaphoreType.DMA((n_rep, heads)),
            pltpu.SemaphoreType.DMA((n_rep, heads)),
        ],
        compiler_params=pltpu.CompilerParams(
            collective_id=0, has_side_effects=True, vmem_limit_bytes=48 * 1024 * 1024
        ),
    )(keys, values, queries, forward_output, output_gradient, log_sum_norm, block_attend_mask)
    return dq, dkv[0], dkv[1]


def solution(mesh):
    in_specs = (
        P(None, "ctx"),
        P(("ctx", "rep"), None),
        P(("ctx", "rep"), None),
        P(None, "ctx"),
        P(None, "ctx"),
        P("ctx", None),
        P("ctx", None, None),
    )
    out_specs = (P("rep", "ctx"), P(("ctx", "rep"), None), P(("ctx", "rep"), None))
    return jax.shard_map(
        on_device, mesh=mesh, in_specs=in_specs, out_specs=out_specs, check_vma=False
    )
```

```python
import functools

import jax
import jax.numpy as jnp
from jax import lax
from jax.experimental import pallas as pl
from jax.experimental.pallas import tpu as pltpu
from jax.sharding import PartitionSpec as P

KEY_VALUE_HEADS = 8
HEAD_SIZE = 128
BLK = 128
MESH = pl.DeviceIdType.MESH
LOG2_E = 1.4426950408889634
MASKED = 1e30
UN = 4
PAIR = 2 * BLK


def partner_of(index, step, count):
    total = 0
    bit = 1
    while bit < count:
        total = total + ((index // bit + step // bit) % 2) * bit
        bit *= 2
    return total


def kernel(
    n_ctx,
    n_rep,
    heads,
    group,
    keys,
    values,
    queries,
    fwd_out,
    grad_out,
    norm_in,
    mask_in,
    dq_out,
    dkv_out,
    q_v,
    o_v,
    g_v,
    qt_v,
    gt_v,
    norm_b,
    dots_b,
    kv_v,
    dk_acc,
    dv_acc,
    dq_acc,
    dkv_send,
    dq_send,
    dq_land,
    dkv_land,
    norm,
    mask,
    load_sem,
    kv_send_sem,
    kv_recv_sem,
    d_send_sem,
    d_recv_sem,
    q_send_sem,
    q_recv_sem,
):
    ctx = lax.axis_index("ctx")
    rep = lax.axis_index("rep")
    n_q = q_v.shape[0]
    rows = n_q // n_rep
    scale = HEAD_SIZE ** (-0.5)

    def head_cols(head):
        return pl.ds(pl.multiple_of(head * HEAD_SIZE, HEAD_SIZE), HEAD_SIZE)

    def half(index):
        return pl.ds(pl.multiple_of((index % 2) * BLK, BLK), BLK)

    def kv_place(source, kind):
        return kv_v.at[source // 2, kind, half(source)]

    my_head = ctx // group
    my_cols = head_cols(my_head)

    loads = [
        pltpu.make_async_copy(keys.at[:, my_cols], kv_place(ctx, 0), load_sem.at[0]),
        pltpu.make_async_copy(values.at[:, my_cols], kv_place(ctx, 1), load_sem.at[1]),
        pltpu.make_async_copy(grad_out, g_v, load_sem.at[2]),
        pltpu.make_async_copy(fwd_out, o_v, load_sem.at[3]),
        pltpu.make_async_copy(queries, q_v, load_sem.at[4]),
        pltpu.make_async_copy(norm_in, norm, load_sem.at[5]),
        pltpu.make_async_copy(mask_in, mask, load_sem.at[6]),
    ]
    for load in loads:
        load.start()

    barrier = pltpu.get_barrier_semaphore()

    @pl.loop(1, n_ctx)
    def _(step):
        peer = partner_of(ctx, step, n_ctx)
        pl.semaphore_signal(barrier, inc=1, device_id=(peer, rep), device_id_type=MESH)

    @pl.loop(1, n_rep)
    def _(step):
        peer = partner_of(rep, step, n_rep)
        pl.semaphore_signal(barrier, inc=1, device_id=(ctx, peer), device_id_type=MESH)

    pl.semaphore_wait(barrier, n_ctx - 1 + n_rep - 1)

    def kv_copy(step, kind):
        peer = partner_of(ctx, step, n_ctx)
        source = (keys, values)[kind]
        return pltpu.make_async_remote_copy(
            src_ref=source.at[:, head_cols(peer // group)],
            dst_ref=kv_place(ctx, kind),
            send_sem=kv_send_sem.at[step, kind],
            recv_sem=kv_recv_sem.at[step, kind],
            device_id=(peer, rep),
            device_id_type=MESH,
        )

    def kv_arrival(step, kind):
        peer = partner_of(ctx, step, n_ctx)
        return pltpu.make_async_remote_copy(
            src_ref=(keys, values)[kind].at[:, my_cols],
            dst_ref=kv_place(peer, kind),
            send_sem=kv_send_sem.at[step, kind],
            recv_sem=kv_recv_sem.at[step, kind],
            device_id=(peer, rep),
            device_id_type=MESH,
        )

    @pl.loop(1, n_ctx)
    def _(step):
        kv_copy(step, 0).start()
        kv_copy(step, 1).start()

    for load in loads:
        load.wait()

    @pl.loop(0, heads)
    def _(head):
        cols = head_cols(head)
        g = g_v[:, cols]
        q = q_v[:, cols]
        dots = jnp.sum(g.astype(jnp.float32) * o_v[:, cols].astype(jnp.float32), axis=1, keepdims=True)
        dots_b[head] = jnp.broadcast_to(dots, (n_q, BLK))
        row = norm[pl.ds(head, 1), :] * LOG2_E
        norm_b[head] = jnp.broadcast_to(row, (BLK, n_q)).T
        qt_v[head] = q.T
        gt_v[head] = g.T
        dq_acc[head] = jnp.zeros((n_q, HEAD_SIZE), jnp.float32)

    def landing(source, kind):
        place = head_cols(source // group)
        if group == 1:
            return dkv_out.at[kind, :, place]
        return dkv_land.at[source % group, kind, :, place]

    def d_copy(step, kind):
        peer = partner_of(ctx, step, n_ctx)
        return pltpu.make_async_remote_copy(
            src_ref=dkv_send.at[step // 2, kind, half(peer)],
            dst_ref=landing(ctx, kind),
            send_sem=d_send_sem.at[step, kind],
            recv_sem=d_recv_sem.at[step, kind],
            device_id=(peer, rep),
            device_id_type=MESH,
        )

    def d_arrival(step, kind):
        peer = partner_of(ctx, step, n_ctx)
        return pltpu.make_async_remote_copy(
            src_ref=dkv_send.at[step // 2, kind, half(peer)],
            dst_ref=landing(peer, kind),
            send_sem=d_send_sem.at[step, kind],
            recv_sem=d_recv_sem.at[step, kind],
            device_id=(peer, rep),
            device_id_type=MESH,
        )

    def q_copy(step, head):
        peer = partner_of(rep, step, n_rep)
        at = pl.ds(pl.multiple_of(peer * rows, rows), rows)
        return pltpu.make_async_remote_copy(
            src_ref=dq_send.at[head, at],
            dst_ref=dq_land.at[step, head],
            send_sem=q_send_sem.at[step, head],
            recv_sem=q_recv_sem.at[step, head],
            device_id=(ctx, peer),
            device_id_type=MESH,
        )

    def compute(turn, head):
        chip = partner_of(ctx // 2, turn, n_ctx // 2)
        cols = head_cols(head)
        k = kv_v[chip, 0]
        v = kv_v[chip, 1]
        q = q_v[:, cols]
        g = g_v[:, cols]
        nt = (((1,), (1,)), ((), ()))
        s = lax.dot_general(q, k, nt, preferred_element_type=jnp.float32)
        gw = lax.dot_general(g, v, nt, preferred_element_type=jnp.float32)
        p_rows, ds_rows = [], []
        for qb in range(n_q // BLK):
            span = slice(qb * BLK, (qb + 1) * BLK)
            p_cols, ds_cols = [], []
            for j in range(2):
                part = slice(j * BLK, (j + 1) * BLK)
                key_block = (2 * chip + j) * n_rep + rep
                off = (1 - mask[head, qb, key_block]).astype(jnp.float32) * MASKED
                w = jnp.exp2(s[span, part] * (scale * LOG2_E) - (norm_b[head, span, :] + off))
                p_cols.append(w.astype(jnp.bfloat16))
                ds_cols.append((w * (gw[span, part] - dots_b[head, span, :])).astype(jnp.bfloat16))
            p_rows.append(jnp.concatenate(p_cols, axis=1))
            ds_rows.append(jnp.concatenate(ds_cols, axis=1))
        p = jnp.concatenate(p_rows, axis=0)
        ds = jnp.concatenate(ds_rows, axis=0)
        dk_acc[...] += jnp.dot(qt_v[head], ds, preferred_element_type=jnp.float32)
        dv_acc[...] += jnp.dot(gt_v[head], p, preferred_element_type=jnp.float32)
        return dq_acc[head] + jnp.dot(ds, k, preferred_element_type=jnp.float32)

    def clear():
        dk_acc[...] = jnp.zeros_like(dk_acc)
        dv_acc[...] = jnp.zeros_like(dv_acc)

    def arrive(step):
        for kind in range(2):
            kv_arrival(step, kind).wait_recv()

    def give_back(turn):
        dkv_send[turn, 0] = (dk_acc[...] * scale).T.astype(jnp.bfloat16)
        dkv_send[turn, 1] = dv_acc[...].T.astype(jnp.bfloat16)

    def send_back(step):
        for kind in range(2):
            d_copy(step, kind).start()

    arrive(1)
    clear()

    @pl.loop(0, heads, unroll=UN)
    def _(head):
        dq_acc[head] = compute(0, head)

    give_back(0)
    send_back(1)
    for kind in range(2):
        own = dkv_send[0, kind, half(ctx), :]
        if group == 1:
            dkv_out[kind, :, my_cols] = own
        else:
            dkv_land[ctx % group, kind, :, my_cols] = own

    @pl.loop(1, n_ctx // 2 - 1)
    def _(turn):
        arrive(2 * turn)
        arrive(2 * turn + 1)
        clear()

        @pl.loop(0, heads, unroll=UN)
        def _(head):
            dq_acc[head] = compute(turn, head)

        give_back(turn)
        send_back(2 * turn)
        send_back(2 * turn + 1)

    last = n_ctx // 2 - 1
    arrive(2 * last)
    arrive(2 * last + 1)
    clear()

    @pl.loop(0, heads, unroll=UN)
    def _(head):
        total = compute(last, head) * scale
        dq_acc[head] = total
        dq_send[head] = total.astype(jnp.bfloat16)

        @pl.loop(1, n_rep)
        def _(step):
            q_copy(step, head).start()

    give_back(last)
    send_back(2 * last)
    send_back(2 * last + 1)

    @pl.loop(1, n_ctx)
    def _(step):
        for kind in range(2):
            kv_copy(step, kind).wait_send()

    at = pl.ds(pl.multiple_of(rep * rows, rows), rows)

    @pl.loop(0, heads)
    def _(head):
        @pl.loop(1, n_rep)
        def _(step):
            q_copy(step, head).wait_recv()

        total = dq_acc[head, at, :]
        for step in range(1, n_rep):
            total = total + dq_land[step, head].astype(jnp.float32)
        dq_out[:, head_cols(head)] = total.astype(jnp.bfloat16)

    @pl.loop(1, n_ctx)
    def _(step):
        for kind in range(2):
            d_copy(step, kind).wait_send()
            d_arrival(step, kind).wait_recv()

    @pl.loop(0, heads)
    def _(head):
        @pl.loop(1, n_rep)
        def _(step):
            q_copy(step, head).wait_send()

    if group > 1:
        for kind in range(2):
            parts = [dkv_land[j, kind] for j in range(group)]
            while len(parts) > 1:
                parts = [
                    (parts[i].astype(jnp.float32) + parts[i + 1].astype(jnp.float32)).astype(jnp.bfloat16)
                    for i in range(0, len(parts), 2)
                ]
            dkv_out[kind] = parts[0]


def on_device(queries, keys, values, forward_output, output_gradient, log_sum_norm, block_attend_mask):
    n_ctx = lax.axis_size("ctx")
    n_rep = lax.axis_size("rep")
    group = n_ctx // KEY_VALUE_HEADS
    n_q, width = queries.shape
    heads = width // HEAD_SIZE
    rows = n_q // n_rep
    share = keys.shape[0]
    assert share == BLK
    hbm = pl.BlockSpec(memory_space=pltpu.HBM)
    vmem = pl.BlockSpec(memory_space=pltpu.VMEM)
    bf16, f32 = jnp.bfloat16, jnp.float32
    land_group = group if group > 1 else 1
    land_cols = keys.shape[1] if group > 1 else HEAD_SIZE
    dq, dkv = pl.pallas_call(
        functools.partial(kernel, n_ctx, n_rep, heads, group),
        out_shape=(
            jax.ShapeDtypeStruct((rows, width), bf16),
            jax.ShapeDtypeStruct((2, share, keys.shape[1]), bf16),
        ),
        in_specs=[hbm] * 7,
        out_specs=(vmem, vmem),
        scratch_shapes=[
            pltpu.VMEM((n_q, width), bf16),
            pltpu.VMEM((n_q, width), bf16),
            pltpu.VMEM((n_q, width), bf16),
            pltpu.VMEM((heads, HEAD_SIZE, n_q), bf16),
            pltpu.VMEM((heads, HEAD_SIZE, n_q), bf16),
            pltpu.VMEM((heads, n_q, BLK), f32),
            pltpu.VMEM((heads, n_q, BLK), f32),
            pltpu.VMEM((n_ctx // 2, 2, PAIR, HEAD_SIZE), bf16),
            pltpu.VMEM((HEAD_SIZE, PAIR), f32),
            pltpu.VMEM((HEAD_SIZE, PAIR), f32),
            pltpu.VMEM((heads, n_q, HEAD_SIZE), f32),
            pltpu.VMEM((n_ctx // 2, 2, PAIR, HEAD_SIZE), bf16),
            pltpu.VMEM((heads, n_q, HEAD_SIZE), bf16),
            pltpu.VMEM((n_rep, heads, rows, HEAD_SIZE), bf16),
            pltpu.VMEM((land_group, 2, BLK, land_cols), bf16),
            pltpu.VMEM(log_sum_norm.shape, f32),
            pltpu.SMEM(block_attend_mask.shape, jnp.int32),
            pltpu.SemaphoreType.DMA((7,)),
            pltpu.SemaphoreType.DMA((n_ctx, 2)),
            pltpu.SemaphoreType.DMA((n_ctx, 2)),
            pltpu.SemaphoreType.DMA((n_ctx, 2)),
            pltpu.SemaphoreType.DMA((n_ctx, 2)),
            pltpu.SemaphoreType.DMA((n_rep, heads)),
            pltpu.SemaphoreType.DMA((n_rep, heads)),
        ],
        compiler_params=pltpu.CompilerParams(
            collective_id=0, has_side_effects=True, vmem_limit_bytes=48 * 1024 * 1024
        ),
    )(keys, values, queries, forward_output, output_gradient, log_sum_norm, block_attend_mask)
    return dq, dkv[0], dkv[1]


def solution(mesh):
    in_specs = (
        P(None, "ctx"),
        P(("ctx", "rep"), None),
        P(("ctx", "rep"), None),
        P(None, "ctx"),
        P(None, "ctx"),
        P("ctx", None),
        P("ctx", None, None),
    )
    out_specs = (P("rep", "ctx"), P(("ctx", "rep"), None), P(("ctx", "rep"), None))
    return jax.shard_map(
        on_device, mesh=mesh, in_specs=in_specs, out_specs=out_specs, check_vma=False
    )
```
